256 devices in a mesh: row: 32 (over y, x, core), col: 8 (over z).
Axes of the slice: x: 4, y: 4, z: 8, core: 2. Of those that a mesh axis runs over, the one named last changes fastest.
Arguments:
- gram: float32 [16384, 16384], P('row', 'col'), may hold values from -70 to 70, as said below
- descriptors: float32 [16384, 2048], P('row', 'col'), may hold values from -0.6 to 0.6
Outputs:
- factored: float32 [16384, 16384], P('row', 'col')
- reduced: float32 [16384, 2048], P('row', 'col')
- variance: float32 [2048], P('col')
The draws below stay inside these ranges and needn't reach their ends.
Inputs may be any that keep to these rules, and one draw needn't show every extreme that they name: `gram`: symmetric positive definite in natural order with a positive diagonal; columns stored as the steps say.
All inputs are finite; a program needn't handle non-finite values.
Results may differ from the reference program's by a relative error of at most 0.0001.
Values sent between devices are 32-bit elements; how exact they have to be, the bound alone decides.
No kernel may reach another device: no remote copies, remote signals or barrier semaphores. Data moves between devices by JAX's collectives and lax.ppermute only.
A program may use at most 128 MiB of HBM per device.

```python
import jax
import jax.numpy as jnp
from jax import lax

NB = 512
PANELS = 2
M = 16384
Q = 2048
N_COL = 8


def draw_gram(key, part):
    key = jax.random.fold_in(key, 11)
    key_scale, key_base, key_factor = jax.random.split(key, 3)
    spread = 0.6
    scales = jnp.exp(jax.random.uniform(key_scale, (M,), jnp.float32, -spread, spread))
    diag_base = jax.random.uniform(key_base, (M,), jnp.float32, 0.5, 1.5)
    factor_rank = 4 * NB
    factor = jax.random.randint(key_factor, (M, factor_rank), -3, 4).astype(jnp.float32).astype(jnp.bfloat16)
    products = jnp.dot(factor, factor.T, preferred_element_type=jnp.float32) / float(factor_rank)
    combined = 0.5 * products + jnp.diag(diag_base)
    natural = scales[:, None] * scales[None, :] * combined
    blocks = M // (N_COL * NB)
    return natural.reshape(M, blocks, N_COL, NB).transpose(0, 2, 1, 3).reshape(M, M).astype(jnp.float32)


def block_levels(rng, shape, cuts, low, high):
    factor_of, own = 1.0, jax.random.fold_in(rng, 6)
    for axis_at, shards_of in cuts:
        heights = jnp.exp(jax.random.uniform(jax.random.fold_in(own, axis_at), (shards_of,), jnp.float32, low / len(cuts), high / len(cuts)))
        factor_of = factor_of * jnp.repeat(heights, shape[axis_at] // shards_of).reshape([-1 if axis == axis_at else 1 for axis in range(len(shape))])
    return factor_of


def gaussian(rng, shape, deviation, limit, shards=(), kind=jnp.bfloat16):
    result = deviation * jax.random.normal(rng, shape, jnp.float32)
    if shards:
        result = result * block_levels(rng, shape, shards, -0.22, 0.18)
    return jnp.clip(result, -limit, limit).astype(kind)


def setup_inputs(seed: int = 0) -> dict:
    splits = jax.random.split(jax.random.key(seed), 3)
    gram = draw_gram(jax.random.fold_in(splits[2], 71), 0)
    descriptors = gaussian(splits[1], (M, Q), 0.1, 0.6, ((0, 32), (1, 8)), jnp.float32)
    return {"gram": gram, "descriptors": descriptors}


def unstore(stored):
    blocks = M // (N_COL * NB)
    return stored.reshape(M, N_COL, blocks, NB).transpose(0, 2, 1, 3).reshape(M, M)

def restore(natural):
    blocks = M // (N_COL * NB)
    return natural.reshape(M, blocks, N_COL, NB).transpose(0, 2, 1, 3).reshape(M, M)

def reference(gram, descriptors):
    matrix = unstore(gram)
    coeffs = descriptors
    variance = jnp.zeros((Q,), jnp.float32)
    for k in range(PANELS):
        start = k * NB
        pivot = jnp.linalg.cholesky(matrix[start:start + NB, start:start + NB])
        below = jax.scipy.linalg.solve_triangular(pivot, matrix[start + NB:, start:start + NB].T, lower=True).T
        panel = jnp.concatenate([jnp.zeros((start, NB), jnp.float32), pivot, below], axis=0)
        solved = jax.scipy.linalg.solve_triangular(pivot, coeffs[start:start + NB], lower=True)
        tail = coeffs[start + NB:] - jnp.dot(below, solved, precision=lax.Precision.HIGHEST)
        coeffs = jnp.concatenate([coeffs[:start], solved, tail], axis=0)
        variance = variance + jnp.sum(solved * solved, axis=0)
        matrix = matrix - jnp.dot(panel, panel.T, precision=lax.Precision.HIGHEST)
        matrix = matrix.at[:, start:start + NB].set(panel)
        matrix = matrix.at[start:start + NB, start + NB:].set(0.0)
    return (restore(matrix), coeffs, variance)
```

```python
import jax
import jax.numpy as jnp
from jax import lax
from jax.experimental import pallas as pl
from jax.experimental.pallas import tpu as pltpu
from jax.sharding import PartitionSpec as P

HIGHEST = lax.Precision.HIGHEST
HIGH = lax.Precision.HIGH
TILE = 128
SUB = 8


def lane_of(x, at):
    return jnp.broadcast_to(x[:, at:at + 1], x.shape)


def sub_of(x, at):
    return jnp.broadcast_to(x[at:at + 1, :], x.shape)


def invert_tile(rows):
    shape = rows[0].shape
    lane = lax.broadcasted_iota(jnp.int32, shape, 1)
    sub = lax.broadcasted_iota(jnp.int32, shape, 0)
    count = len(rows)
    for p in range(count):
        at = SUB * p
        panel = (lane >= at) & (lane < at + SUB)
        row = rows[p]
        diag = [lane_of(row, at + k) for k in range(SUB)]
        row = jnp.where(panel, jnp.where(lane == sub + at, 1.0, 0.0), row)
        inv, tops, low = [], [], {}
        for k in range(SUB):
            scale = lax.rsqrt(sub_of(diag[k], k))
            inv.append(scale)
            mult = diag[k] * scale
            top = sub_of(row, k) * scale
            tops.append(top)
            for j in range(k + 1, SUB):
                low[j, k] = sub_of(diag[j], k) * scale
                diag[j] = diag[j] - mult * low[j, k]
            row = row - mult * top
        done = tops[0]
        for k in range(1, SUB):
            done = jnp.where(sub == k, tops[k], done)
        rows[p] = jnp.where(lane <= sub + at, done, 0.0)
        for i in range(p + 1, count):
            cols = [lane_of(rows[i], at + k) for k in range(SUB)]
            rest = jnp.where(panel, 0.0, rows[i])
            for k in range(SUB):
                mult = cols[k] * inv[k]
                for j in range(k + 1, SUB):
                    cols[j] = cols[j] - mult * low[j, k]
                rest = rest - mult * tops[k]
            rows[i] = rest
    return jnp.concatenate(rows, axis=0)


def factor_kernel(a_ref, t_ref):
    count = a_ref.shape[0] // TILE
    t_ref[...] = a_ref[...]

    def block(i):
        return pl.ds(pl.multiple_of(i * TILE, TILE), TILE)

    def step(j, carry):
        here = block(j)
        rows = [
            t_ref[pl.ds(pl.multiple_of(j * TILE + SUB * i, SUB), SUB), here]
            for i in range(TILE // SUB)
        ]
        tile = invert_tile(rows)
        t_ref[here, :] = jnp.dot(tile, t_ref[here, :], precision=HIGHEST)
        lefts = t_ref[here, :]
        t_ref[here, here] = tile

        def below(i, carry):
            there = block(i)
            left = t_ref[here, there]
            t_ref[there, here] = jnp.zeros((TILE, TILE), jnp.float32)
            t_ref[there, :] -= lax.dot_general(
                left, t_ref[here, :], (((0,), (0,)), ((), ())), precision=HIGHEST,
                preferred_element_type=jnp.float32,
            )
            return carry

        return lax.fori_loop(j + 1, count, below, carry)

    lax.fori_loop(0, count, step, 0)


def factor_inverse(a):
    order = a.shape[0]
    return pl.pallas_call(
        factor_kernel,
        out_shape=jax.ShapeDtypeStruct(a.shape, jnp.float32),
        in_specs=[pl.BlockSpec(memory_space=pltpu.VMEM)],
        out_specs=pl.BlockSpec(memory_space=pltpu.VMEM),
        compiler_params=pltpu.CompilerParams(vmem_limit_bytes=40 * 2**20),
        cost_estimate=pl.CostEstimate(flops=6 * order**3, bytes_accessed=8 * order * order, transcendentals=order),
        name="factor_inverse",
    )(a)


def mesh_shapes():
    return lax.axis_size("row"), lax.axis_size("col")


def body(gram, desc):
    nb = gram.shape[0]
    stored = gram.shape[1]
    nrow, ncol = mesh_shapes()
    groups = nrow // ncol
    order = 2 * nb
    prow = lax.axis_index("row")
    pcol = lax.axis_index("col")
    slab = nb // ncol
    panel = gram[:, :nb]

    got = lax.all_to_all(panel.reshape(ncol, slab, nb), "col", 0, 0, tiled=True)
    rows_slab = jnp.concatenate([got[0], got[1]], axis=1)

    tiles = rows_slab.reshape(slab // 8, 8, order // 256, 256).transpose(0, 2, 1, 3)
    tiles = tiles.reshape(nrow, 8, 256)
    dealt = lax.all_to_all(tiles, "row", 0, 0, tiled=True)[:2]
    lead = lax.all_gather(dealt, "col")
    lead = lax.all_to_all(
        jnp.broadcast_to(lead[None], (nrow,) + lead.shape), "row", 0, 0, tiled=True
    )
    lead = lead.reshape(slab // 8, order // 256, ncol, 2, 8, 256)
    lead = lead.transpose(3, 2, 0, 4, 1, 5).reshape(order, order)

    mine = lax.all_gather(rows_slab, "col", tiled=True)
    halves = [None, None]
    inner = prow % ncol
    pieces = panel.reshape(ncol, slab, nb)
    got0 = jnp.zeros((slab, nb), jnp.float32)
    got1 = jnp.zeros((slab, nb), jnp.float32)
    for s in range(ncol):
        pairs = []
        for y in range(groups):
            for i in range(ncol):
                pairs.append(((y * ncol + i) * ncol, (y * ncol + (i + s) % ncol) * ncol + i))
                pairs.append(
                    ((y * ncol + i) * ncol + 1, (y * ncol + (i + s + ncol // 2) % ncol) * ncol + i)
                )
        which = (inner + s + jnp.where(pcol == 0, 0, ncol // 2)) % ncol
        piece = lax.dynamic_index_in_dim(pieces, which, 0, keepdims=False)
        come = lax.ppermute(piece, ("row", "col"), pairs)
        got0 = jnp.where((inner - pcol - s) % ncol == 0, come, got0)
        got1 = jnp.where((inner - pcol - s - ncol // 2) % ncol == 0, come, got1)
    match = lax.all_gather(jnp.concatenate([got0, got1], axis=1), "row", tiled=True)

    chunk = desc.shape[0] // nrow
    head = lax.all_to_all(desc.reshape(nrow, chunk, -1), "row", 0, 0, tiled=True)[:2]
    head = lax.all_gather(head, "row")
    head = head.transpose(1, 0, 2, 3).reshape(order, -1)

    inverse = factor_inverse(lead)
    lower = jnp.where(
        lax.broadcasted_iota(jnp.int32, (order, order), 0)
        >= lax.broadcasted_iota(jnp.int32, (order, order), 1),
        inverse, 0.0,
    )
    solved = lax.dot_general(mine, lower, (((1,), (1,)), ((), ())), precision=HIGHEST)
    weights = jnp.dot(solved, lower, precision=HIGHEST)
    update = lax.dot_general(weights, match, (((1,), (1,)), ((), ())), precision=HIGH)
    z = jnp.dot(lower, head, precision=HIGHEST)
    variance = jnp.sum(z * z, axis=0)
    lowered = desc - jnp.dot(weights, head, precision=HIGH)
    reduced = jnp.where(prow == 0, z[:nb], jnp.where(prow == 1, z[nb:], lowered))

    row_at = prow * nb + lax.broadcasted_iota(jnp.int32, (nb, nb), 0)
    col_at = pcol * nb + lax.broadcasted_iota(jnp.int32, (nb, nb), 1)
    factor = jnp.where(pcol == 0, solved[:, :nb], solved[:, nb:])
    factor = jnp.where(row_at >= col_at, factor, 0.0)
    rest = jnp.where(prow < 2, 0.0, gram - update)
    rest = rest.at[:, :nb].set(jnp.where(pcol < 2, factor, rest[:, :nb]))
    return (rest, reduced, variance)


def solution(mesh):
    in_specs = (P("row", "col"), P("row", "col"))
    out_specs = (P("row", "col"), P("row", "col"), P("col"))
    return jax.shard_map(body, mesh=mesh, in_specs=in_specs, out_specs=out_specs, check_vma=False)
```

```python
import jax
import jax.numpy as jnp
from jax import lax
from jax.experimental import pallas as pl
from jax.experimental.pallas import tpu as pltpu
from jax.sharding import PartitionSpec as P

HIGHEST = lax.Precision.HIGHEST
HIGH = lax.Precision.HIGH
TILE = 128
SUB = 8


def lane_of(x, at):
    return jnp.broadcast_to(x[:, at:at + 1], x.shape)


def sub_of(x, at):
    return jnp.broadcast_to(x[at:at + 1, :], x.shape)


def invert_tile(rows):
    shape = rows[0].shape
    lane = lax.broadcasted_iota(jnp.int32, shape, 1)
    sub = lax.broadcasted_iota(jnp.int32, shape, 0)
    count = len(rows)
    for p in range(count):
        at = SUB * p
        panel = (lane >= at) & (lane < at + SUB)
        row = rows[p]
        diag = [lane_of(row, at + k) for k in range(SUB)]
        row = jnp.where(panel, jnp.where(lane == sub + at, 1.0, 0.0), row)
        inv, tops, low = [], [], {}
        for k in range(SUB):
            scale = lax.rsqrt(sub_of(diag[k], k))
            inv.append(scale)
            mult = diag[k] * scale
            top = sub_of(row, k) * scale
            tops.append(top)
            for j in range(k + 1, SUB):
                low[j, k] = sub_of(diag[j], k) * scale
                diag[j] = diag[j] - mult * low[j, k]
            row = row - mult * top
        done = tops[0]
        for k in range(1, SUB):
            done = jnp.where(sub == k, tops[k], done)
        rows[p] = jnp.where(lane <= sub + at, done, 0.0)
        for i in range(p + 1, count):
            cols = [lane_of(rows[i], at + k) for k in range(SUB)]
            rest = jnp.where(panel, 0.0, rows[i])
            for k in range(SUB):
                mult = cols[k] * inv[k]
                for j in range(k + 1, SUB):
                    cols[j] = cols[j] - mult * low[j, k]
                rest = rest - mult * tops[k]
            rows[i] = rest
    return jnp.concatenate(rows, axis=0)


def block(i):
    return pl.ds(pl.multiple_of(i * TILE, TILE), TILE)


def factor_in_place(t_ref):
    count = t_ref.shape[0] // TILE

    def step(j, carry):
        here = block(j)
        rows = [
            t_ref[pl.ds(pl.multiple_of(j * TILE + SUB * i, SUB), SUB), here]
            for i in range(TILE // SUB)
        ]
        tile = invert_tile(rows)
        t_ref[here, :] = jnp.dot(tile, t_ref[here, :], precision=HIGHEST)
        t_ref[here, here] = tile

        def below(i, carry):
            there = block(i)
            left = t_ref[here, there]
            t_ref[there, here] = jnp.zeros((TILE, TILE), jnp.float32)
            t_ref[there, :] -= lax.dot_general(
                left, t_ref[here, :], (((0,), (0,)), ((), ())), precision=HIGHEST,
                preferred_element_type=jnp.float32,
            )
            return carry

        return lax.fori_loop(j + 1, count, below, carry)

    lax.fori_loop(0, count, step, 0)


def mask_lower(t_ref):
    order = t_ref.shape[0]
    for j in range(order // TILE - 1):
        t_ref[j * TILE:(j + 1) * TILE, (j + 1) * TILE:] = jnp.zeros(
            (TILE, order - (j + 1) * TILE), jnp.float32
        )


def tile_home(q, c, core, nb, ncol):
    slab = nb // ncol
    pairs = nb // TILE // 2
    row = c * slab + (q // pairs) * SUB
    col = (q % pairs) * 2 * TILE + core * TILE
    return slice(row, row + SUB), pl.ds(pl.multiple_of(col, TILE), TILE)


def first_kernel(core_ref, own_ref, other_ref, t_ref):
    core = core_ref[0]
    nb = t_ref.shape[0]
    count, ncol = own_ref.shape[:2]
    for q in range(count):
        for c in range(ncol):
            t_ref[tile_home(q, c, core, nb, ncol)] = own_ref[q, c]
            t_ref[tile_home(q, c, 1 - core, nb, ncol)] = other_ref[q, c]
    factor_in_place(t_ref)
    mask_lower(t_ref)


def second_kernel(core_ref, own_ref, other_ref, first_ref, out_ref, left_ref, t_ref):
    core = core_ref[0]
    nb = t_ref.shape[0]
    count, ncol = own_ref.shape[:2]
    for q in range(count):
        for c in range(ncol):
            here = tile_home(q, c, core, nb, ncol)
            there = tile_home(q, c, 1 - core, nb, ncol)
            left_ref[here] = own_ref[q, c, 0]
            left_ref[there] = other_ref[q, c, 0]
            t_ref[here] = own_ref[q, c, 1]
            t_ref[there] = other_ref[q, c, 1]
    first = first_ref[...]
    left = lax.dot_general(
        left_ref[...], first, (((1,), (1,)), ((), ())), precision=HIGHEST,
        preferred_element_type=jnp.float32,
    )
    left_ref[...] = left
    t_ref[...] -= lax.dot_general(
        left, left, (((1,), (1,)), ((), ())), precision=HIGHEST,
        preferred_element_type=jnp.float32,
    )
    factor_in_place(t_ref)
    mask_lower(t_ref)
    out_ref[:nb, :nb] = first
    out_ref[:nb, nb:] = jnp.zeros((nb, nb), jnp.float32)
    out_ref[nb:, nb:] = t_ref[...]
    left_ref[...] = jnp.dot(left_ref[...], first, precision=HIGHEST)
    out_ref[nb:, :nb] = -jnp.dot(t_ref[...], left_ref[...], precision=HIGHEST)


VMEM = pl.BlockSpec(memory_space=pltpu.VMEM)
SMEM = pl.BlockSpec(memory_space=pltpu.SMEM)


def factor_first(core, own, other, nb):
    return pl.pallas_call(
        first_kernel,
        out_shape=jax.ShapeDtypeStruct((nb, nb), jnp.float32),
        in_specs=[SMEM, VMEM, VMEM],
        out_specs=VMEM,
        compiler_params=pltpu.CompilerParams(vmem_limit_bytes=24 * 2**20),
        cost_estimate=pl.CostEstimate(flops=150 * nb**3, bytes_accessed=8 * nb * nb, transcendentals=0),
        name="factor_first",
    )(core, own, other)


def factor_second(core, own, other, first):
    nb = first.shape[0]
    return pl.pallas_call(
        second_kernel,
        out_shape=jax.ShapeDtypeStruct((2 * nb, 2 * nb), jnp.float32),
        in_specs=[SMEM, VMEM, VMEM, VMEM],
        out_specs=VMEM,
        scratch_shapes=[pltpu.VMEM((nb, nb), jnp.float32)] * 2,
        compiler_params=pltpu.CompilerParams(vmem_limit_bytes=32 * 2**20),
        cost_estimate=pl.CostEstimate(flops=200 * nb**3, bytes_accessed=28 * nb * nb, transcendentals=0),
        name="factor_second",
    )(core, own, other, first)


def spread(x, axis, groups=None):
    size = lax.axis_size(axis) if groups is None else len(groups[0])
    return lax.all_to_all(
        jnp.broadcast_to(x[None], (size,) + x.shape), axis, 0, 0, tiled=True,
        axis_index_groups=groups,
    )


def body(gram, desc):
    nb = gram.shape[0]
    qn = desc.shape[1]
    nrow, ncol = lax.axis_size("row"), lax.axis_size("col")
    groups = nrow // ncol
    order = 2 * nb
    prow = lax.axis_index("row")
    pcol = lax.axis_index("col")
    core = prow % 2
    slab = nb // ncol
    wide = nb // TILE
    lanes = [[2 * q + k for q in range(nrow // 2)] for k in range(2)]
    swap = [(r, r ^ 1) for r in range(nrow)]
    panel = gram[:, :nb]

    got = lax.all_to_all(panel.reshape(ncol, slab, nb), "col", 0, 0, tiled=True)
    rows_slab = jnp.concatenate([got[0], got[1]], axis=1)

    half = groups // 2
    pairs = []
    for y in range(groups):
        for i in range(ncol):
            for c in range(ncol):
                to = 2 * ((y % half) * ncol + c) + y // half
                pairs.append(((y * ncol + i) * ncol + c, to * ncol + i))
    match = lax.ppermute(rows_slab, ("row", "col"), pairs)
    match = lax.all_gather(match, "row", axis_index_groups=lanes, tiled=True)

    tiles = rows_slab.reshape(slab // SUB, SUB, 2, wide, TILE).transpose(0, 3, 2, 1, 4)
    tiles = tiles.reshape(nrow, 2, SUB, TILE)
    chunk = nb // nrow
    heads = desc.reshape(nrow, chunk // SUB, SUB, qn // TILE, TILE).transpose(0, 1, 3, 2, 4)
    heads = heads.reshape(nrow, -1, SUB, TILE)
    dealt = lax.all_to_all(jnp.concatenate([tiles, heads], axis=1), "row", 0, 0, tiled=True)
    lead = spread(jnp.concatenate([dealt[0, :1], dealt[1, :2]], axis=0), "col")

    come = [
        lax.ppermute(rows_slab, "col", [(c, (c + s) % ncol) for c in range(ncol)])
        for s in range(1, ncol)
    ]

    lead_own = spread(lead[:, 0], "row", lanes)
    lead_other = lax.ppermute(lead_own, "row", swap)
    next_own = spread(lead[:, 1:], "row", lanes)
    index = core.astype(jnp.int32).reshape(1)
    first = factor_first(index, lead_own, lead_other, nb)

    heads = dealt[:2, 2:]
    first, next_own, heads, come = lax.optimization_barrier((first, next_own, heads, come))
    next_other = lax.ppermute(next_own, "row", swap)
    head = spread(heads, "row").reshape(nrow, 2, chunk // SUB, qn // TILE, SUB, TILE)
    head = head.transpose(1, 0, 2, 4, 3, 5).reshape(order, qn)
    mine = jnp.zeros((nb, order), jnp.float32)
    mine = lax.dynamic_update_slice(mine, rows_slab, (pcol * slab, 0))
    for s in range(1, ncol):
        mine = lax.dynamic_update_slice(mine, come[s - 1], ((pcol - s) % ncol * slab, 0))

    lower = factor_second(index, next_own, next_other, first)
    lower, match = lax.optimization_barrier((lower, match))
    other = lax.ppermute(match, "row", swap)
    solved = lax.dot_general(mine, lower, (((1,), (1,)), ((), ())), precision=HIGH)
    weights = jnp.dot(solved, lower, precision=HIGH)
    z = jnp.dot(lower, head, precision=HIGHEST)
    variance = jnp.sum(z * z, axis=0)
    lowered = desc - jnp.dot(weights, head, precision=HIGH)
    reduced = jnp.where(prow == 0, z[:nb], jnp.where(prow == 1, z[nb:], lowered))

    own = lax.dot_general(weights, match, (((1,), (1,)), ((), ())), precision=HIGH)
    other = lax.dot_general(weights, other, (((1,), (1,)), ((), ())), precision=HIGH)
    update = jnp.concatenate(
        [jnp.where(core == 0, own, other), jnp.where(core == 0, other, own)], axis=1
    )
    row_at = prow * nb + lax.broadcasted_iota(jnp.int32, (nb, nb), 0)
    col_at = pcol * nb + lax.broadcasted_iota(jnp.int32, (nb, nb), 1)
    factor = jnp.where(pcol == 0, solved[:, :nb], solved[:, nb:])
    factor = jnp.where(row_at >= col_at, factor, 0.0)
    rest = jnp.where(prow < 2, 0.0, gram - update)
    rest = rest.at[:, :nb].set(jnp.where(pcol < 2, factor, rest[:, :nb]))
    return (rest, reduced, variance)


def solution(mesh):
    in_specs = (P("row", "col"), P("row", "col"))
    out_specs = (P("row", "col"), P("row", "col"), P("col"))
    return jax.shard_map(body, mesh=mesh, in_specs=in_specs, out_specs=out_specs, check_vma=False)
```

```python
import functools

import jax
import jax.numpy as jnp
from jax import lax
from jax.experimental import pallas as pl
from jax.experimental.pallas import tpu as pltpu
from jax.sharding import PartitionSpec as P

HIGHEST = lax.Precision.HIGHEST
TILE = 128
SUB = 8


def lane_of(x, at):
    return jnp.broadcast_to(x[:, at:at + 1], x.shape)


def sub_of(x, at):
    return jnp.broadcast_to(x[at:at + 1, :], x.shape)


def invert_tile(rows):
    shape = rows[0].shape
    lane = lax.broadcasted_iota(jnp.int32, shape, 1)
    sub = lax.broadcasted_iota(jnp.int32, shape, 0)
    count = len(rows)
    for p in range(count):
        at = SUB * p
        panel = (lane >= at) & (lane < at + SUB)
        row = rows[p]
        diag = [lane_of(row, at + k) for k in range(SUB)]
        row = jnp.where(panel, jnp.where(lane == sub + at, 1.0, 0.0), row)
        inv, tops, low = [], [], {}
        for k in range(SUB):
            scale = lax.rsqrt(sub_of(diag[k], k))
            inv.append(scale)
            mult = diag[k] * scale
            top = sub_of(row, k) * scale
            tops.append(top)
            for j in range(k + 1, SUB):
                low[j, k] = sub_of(diag[j], k) * scale
                diag[j] = diag[j] - mult * low[j, k]
            row = row - mult * top
        done = tops[0]
        for k in range(1, SUB):
            done = jnp.where(sub == k, tops[k], done)
        rows[p] = jnp.where(lane <= sub + at, done, 0.0)
        for i in range(p + 1, count):
            cols = [lane_of(rows[i], at + k) for k in range(SUB)]
            rest = jnp.where(panel, 0.0, rows[i])
            for k in range(SUB):
                mult = cols[k] * inv[k]
                for j in range(k + 1, SUB):
                    cols[j] = cols[j] - mult * low[j, k]
                rest = rest - mult * tops[k]
            rows[i] = rest
    return jnp.concatenate(rows, axis=0)


def block(i):
    return pl.ds(pl.multiple_of(i * TILE, TILE), TILE)


def factor_in_place(t_ref):
    count = t_ref.shape[0] // TILE

    def step(j, carry):
        here = block(j)
        rows = [
            t_ref[pl.ds(pl.multiple_of(j * TILE + SUB * i, SUB), SUB), here]
            for i in range(TILE // SUB)
        ]
        tile = invert_tile(rows)
        t_ref[here, :] = jnp.dot(tile, t_ref[here, :], precision=HIGHEST)
        t_ref[here, here] = tile

        def below(i, carry):
            there = block(i)
            left = t_ref[here, there]
            t_ref[there, here] = jnp.zeros((TILE, TILE), jnp.float32)
            t_ref[there, :] -= lax.dot_general(
                left, t_ref[here, :], (((0,), (0,)), ((), ())), precision=HIGHEST,
                preferred_element_type=jnp.float32,
            )
            return carry

        return lax.fori_loop(j + 1, count, below, carry)

    lax.fori_loop(0, count, step, 0)


def mask_lower(t_ref):
    order = t_ref.shape[0]
    for j in range(order // TILE - 1):
        t_ref[j * TILE:(j + 1) * TILE, (j + 1) * TILE:] = jnp.zeros(
            (TILE, order - (j + 1) * TILE), jnp.float32
        )


def split(x):
    high = x.astype(jnp.bfloat16)
    return high, (x - high.astype(jnp.float32)).astype(jnp.bfloat16)


def dot3(left, right, dims):
    def one(x, y):
        return lax.dot_general(x, y, (dims, ((), ())), preferred_element_type=jnp.float32)
    return one(left[0], right[1]) + one(left[1], right[0]) + one(left[0], right[0])


NN = ((1,), (0,))
NT = ((1,), (1,))


def tile_home(q, c, core, nb, ncol):
    slab = nb // ncol
    pairs = nb // TILE // 2
    row = c * slab + (q // pairs) * SUB
    col = (q % pairs) * 2 * TILE + core * TILE
    return slice(row, row + SUB), pl.ds(pl.multiple_of(col, TILE), TILE)


def first_kernel(core_ref, own_ref, other_ref, t_ref):
    core = core_ref[0]
    nb = t_ref.shape[0]
    count, ncol = own_ref.shape[:2]
    for q in range(count):
        for c in range(ncol):
            t_ref[tile_home(q, c, core, nb, ncol)] = own_ref[q, c]
            t_ref[tile_home(q, c, 1 - core, nb, ncol)] = other_ref[q, c]
    factor_in_place(t_ref)
    mask_lower(t_ref)


def second_kernel(at_ref, own_ref, other_ref, first_ref, mine_ref, desc_ref,
                  panel_ref, high_ref, low_ref, reduced_ref, var_ref,
                  left_ref, t_ref, x_ref):
    core, prow, pcol = at_ref[0], at_ref[1], at_ref[2]
    nb = t_ref.shape[0]
    qn = x_ref.shape[1]
    count = own_ref.shape[0]
    ncol = nb // SUB // SUB
    for q in range(count):
        for c in range(ncol):
            here = tile_home(q, c, core, nb, ncol)
            there = tile_home(q, c, 1 - core, nb, ncol)
            left_ref[here] = own_ref[q, 2 * c]
            left_ref[there] = other_ref[q, 2 * c]
            t_ref[here] = own_ref[q, 2 * c + 1]
            t_ref[there] = other_ref[q, 2 * c + 1]
        chunk = nb // count // 2
        for t in range(own_ref.shape[1] - 2 * ncol):
            part, tile = divmod(t, chunk // SUB * (qn // TILE))
            row = part * nb + 2 * q * chunk + tile // (qn // TILE) * SUB
            cols = slice(tile % (qn // TILE) * TILE, (tile % (qn // TILE) + 1) * TILE)
            here = pl.ds(pl.multiple_of(row + core * chunk, SUB), SUB)
            there = pl.ds(pl.multiple_of(row + (1 - core) * chunk, SUB), SUB)
            x_ref[here, cols] = own_ref[q, 2 * ncol + t]
            x_ref[there, cols] = other_ref[q, 2 * ncol + t]
    first = first_ref[...]
    left = lax.dot_general(
        left_ref[...], first, (NT, ((), ())), precision=HIGHEST,
        preferred_element_type=jnp.float32,
    )
    left_ref[...] = left
    t_ref[...] -= lax.dot_general(
        left, left, (NT, ((), ())), precision=HIGHEST, preferred_element_type=jnp.float32,
    )
    factor_in_place(t_ref)
    mask_lower(t_ref)
    left_ref[...] = jnp.dot(left_ref[...], first_ref[...], precision=HIGHEST)
    left_ref[...] = -jnp.dot(t_ref[...], left_ref[...], precision=HIGHEST)

    l00 = split(first_ref[...])
    l10 = split(left_ref[...])
    l11 = split(t_ref[...])
    m0 = split(mine_ref[:, :nb])
    m1 = split(mine_ref[:, nb:])
    p0 = dot3(m0, l00, NT)
    p1 = dot3(m0, l10, NT) + dot3(m1, l11, NT)
    row = prow * nb + lax.broadcasted_iota(jnp.int32, (nb, nb), 0)
    col = pcol * nb + lax.broadcasted_iota(jnp.int32, (nb, nb), 1)
    panel_ref[...] = jnp.where(row >= col, jnp.where(pcol == 0, p0, p1), 0.0)
    p0, p1 = split(p0), split(p1)
    w0 = split(dot3(p0, l00, NN) + dot3(p1, l10, NN))
    w1 = split(dot3(p1, l11, NN))
    high_ref[:, :nb] = w0[0]
    low_ref[:, :nb] = w0[1]
    high_ref[:, nb:] = w1[0]
    low_ref[:, nb:] = w1[1]
    x0 = split(x_ref[:nb])
    x1 = split(x_ref[nb:])
    z0 = dot3(l00, x0, NN)
    z1 = dot3(l10, x0, NN) + dot3(l11, x1, NN)
    var_ref[...] = jnp.sum(z0 * z0, axis=0, keepdims=True) + jnp.sum(z1 * z1, axis=0, keepdims=True)
    lowered = desc_ref[...] - (dot3(w0, x0, NN) + dot3(w1, x1, NN))
    reduced_ref[...] = jnp.where(prow == 0, z0, jnp.where(prow == 1, z1, lowered))


VMEM = pl.BlockSpec(memory_space=pltpu.VMEM)
SMEM = pl.BlockSpec(memory_space=pltpu.SMEM)


def factor_first(core, own, other, nb):
    return pl.pallas_call(
        first_kernel,
        out_shape=jax.ShapeDtypeStruct((nb, nb), jnp.float32),
        in_specs=[SMEM, VMEM, VMEM],
        out_specs=VMEM,
        compiler_params=pltpu.CompilerParams(vmem_limit_bytes=24 * 2**20),
        cost_estimate=pl.CostEstimate(flops=150 * nb**3, bytes_accessed=8 * nb * nb, transcendentals=0),
        name="factor_first",
    )(core, own, other)


def factor_second(at, own, other, first, mine, desc):
    nb, order = mine.shape
    qn = desc.shape[1]
    return pl.pallas_call(
        second_kernel,
        out_shape=(
            jax.ShapeDtypeStruct((nb, nb), jnp.float32),
            jax.ShapeDtypeStruct((nb, order), jnp.bfloat16),
            jax.ShapeDtypeStruct((nb, order), jnp.bfloat16),
            jax.ShapeDtypeStruct((nb, qn), jnp.float32),
            jax.ShapeDtypeStruct((1, qn), jnp.float32),
        ),
        in_specs=[SMEM] + [VMEM] * 5,
        out_specs=(VMEM,) * 5,
        scratch_shapes=[pltpu.VMEM((nb, nb), jnp.float32)] * 2 + [pltpu.VMEM((order, qn), jnp.float32)],
        compiler_params=pltpu.CompilerParams(vmem_limit_bytes=60 * 2**20),
        cost_estimate=pl.CostEstimate(flops=300 * nb**3, bytes_accessed=40 * nb * nb, transcendentals=0),
        name="factor_second",
    )(at, own, other, first, mine, desc)


WIDTH = 256


def update_kernel(flip, at_ref, gram_ref, match_ref, high_ref, low_ref, panel_ref, *refs):
    out_ref = refs[-1]
    prow, pcol = at_ref[1], at_ref[2]
    nb = gram_ref.shape[0]
    steps = pl.num_programs(0)
    half = at_ref[0] if not flip else 1 - at_ref[0]
    tile = half * steps + pl.program_id(0)
    is_panel = (pcol < 2) & (tile < nb // WIDTH)

    @pl.when(is_panel)
    def _():
        out_ref[...] = panel_ref[:, pl.ds(pl.multiple_of(tile * WIDTH, WIDTH), WIDTH)]

    @pl.when(jnp.logical_not(is_panel) & (prow < 2))
    def _():
        out_ref[...] = jnp.zeros((nb, WIDTH), jnp.float32)

    @pl.when(jnp.logical_not(is_panel) & (prow >= 2))
    def _():
        match = split(match_ref[...])
        out_ref[...] = gram_ref[...] - dot3((high_ref[...], low_ref[...]), match, NT)


def update(at, gram, match, high, low, panel, done=None):
    nb, stored = gram.shape
    order = high.shape[1]
    steps = stored // 2 // WIDTH
    flip = done is not None

    def place(t, at_ref):
        half = 1 - at_ref[0] if flip else at_ref[0]
        return (0, half * steps + t)

    whole = pl.BlockSpec((nb, order), lambda t, at_ref: (0, 0))
    in_specs = [
        pl.BlockSpec((nb, WIDTH), place),
        pl.BlockSpec((WIDTH, order), lambda t, at_ref: (t, 0)),
        whole, whole, pl.BlockSpec((nb, nb), lambda t, at_ref: (0, 0)),
    ]
    args = [gram, match, high, low, panel]
    if flip:
        in_specs.append(pl.BlockSpec(memory_space=pl.ANY))
        args.append(done)
    return pl.pallas_call(
        functools.partial(update_kernel, flip),
        grid_spec=pltpu.PrefetchScalarGridSpec(
            num_scalar_prefetch=1,
            grid=(steps,),
            in_specs=in_specs,
            out_specs=pl.BlockSpec((nb, WIDTH), place),
        ),
        out_shape=jax.ShapeDtypeStruct((nb, stored), jnp.float32),
        input_output_aliases={6: 0} if flip else {},
        compiler_params=pltpu.CompilerParams(vmem_limit_bytes=60 * 2**20),
        cost_estimate=pl.CostEstimate(
            flops=6 * nb * stored * order // 2, bytes_accessed=4 * nb * stored + 2 * stored * order,
            transcendentals=0,
        ),
        name="update_other" if flip else "update_own",
    )(at, *args)


def spread(x, axis, groups=None):
    size = lax.axis_size(axis) if groups is None else len(groups[0])
    return lax.all_to_all(
        jnp.broadcast_to(x[None], (size,) + x.shape), axis, 0, 0, tiled=True,
        axis_index_groups=groups,
    )


def body(gram, desc):
    nb = gram.shape[0]
    qn = desc.shape[1]
    nrow, ncol = lax.axis_size("row"), lax.axis_size("col")
    groups = nrow // ncol
    order = 2 * nb
    prow = lax.axis_index("row")
    pcol = lax.axis_index("col")
    core = prow % 2
    slab = nb // ncol
    wide = nb // TILE
    lanes = [[2 * q + k for q in range(nrow // 2)] for k in range(2)]
    swap = [(r, r ^ 1) for r in range(nrow)]
    front = gram[:, :nb]

    chunk = nb // nrow
    heads = desc.reshape(nrow, chunk // SUB, SUB, qn // TILE, TILE).transpose(0, 1, 3, 2, 4)
    heads = heads.reshape(nrow, -1, SUB, TILE)
    heads = lax.all_to_all(heads, "row", 0, 0, tiled=True)

    front = front.reshape(ncol, slab, nb)
    slab0 = jnp.where(pcol == 0, front[0], 0.0)
    slab1 = jnp.where(pcol == 1, front[1], 0.0)
    for s in range(1, ncol):
        piece = jnp.where(pcol == 0, front[s], front[(s + 1) % ncol])
        come = lax.ppermute(piece, "col", [(0, s), (1, (s + 1) % ncol)])
        slab0 = jnp.where(pcol == s, come, slab0)
        slab1 = jnp.where(pcol == (s + 1) % ncol, come, slab1)
    heads, slab0, slab1 = lax.optimization_barrier((heads, slab0, slab1))
    rows_slab = jnp.concatenate([slab0, slab1], axis=1)

    mine = lax.all_gather(rows_slab, "col", tiled=True)

    tiles = rows_slab.reshape(slab // SUB, SUB, 2, wide, TILE).transpose(0, 3, 2, 1, 4)
    tiles = tiles.reshape(nrow, 2, SUB, TILE)
    dealt = lax.all_to_all(tiles, "row", 0, 0, tiled=True)

    half = groups // 2
    pairs = []
    for y in range(groups):
        for i in range(ncol):
            for c in range(ncol):
                to = 2 * ((y % half) * ncol + c) + y // half
                pairs.append(((y * ncol + i) * ncol + c, to * ncol + i))
    match = lax.ppermute(rows_slab, ("row", "col"), pairs)

    lead = spread(jnp.concatenate([dealt[0, :1], dealt[1]], axis=0), "col")

    match, lead = lax.optimization_barrier((match, lead))
    lead_own = spread(lead[:, 0], "row", lanes)
    match = lax.all_gather(match, "row", axis_index_groups=lanes, tiled=True)
    lead_other = lax.ppermute(lead_own, "row", swap)
    following = jnp.concatenate(
        [lead[:, 1:].reshape(2 * ncol, SUB, TILE), heads[0], heads[1]], axis=0
    )
    next_own = spread(following, "row", lanes)
    lead_own, mine = lax.optimization_barrier((lead_own, mine))
    index = jnp.stack([core, prow, pcol]).astype(jnp.int32)
    first = factor_first(index, lead_own, lead_other, nb)

    first, next_own = lax.optimization_barrier((first, next_own))
    next_other = lax.ppermute(next_own, "row", swap)
    panel, high, low, reduced, variance = factor_second(
        index, next_own, next_other, first, mine, desc
    )

    high, match = lax.optimization_barrier((high, match))
    other = lax.ppermute(match, "row", swap)
    rest = update(index, gram, match, high, low, panel)
    rest = update(index, gram, other, high, low, panel, rest)
    return (rest, reduced, variance.reshape(qn))


def solution(mesh):
    in_specs = (P("row", "col"), P("row", "col"))
    out_specs = (P("row", "col"), P("row", "col"), P("col"))
    return jax.shard_map(body, mesh=mesh, in_specs=in_specs, out_specs=out_specs, check_vma=False)
```

```python
import functools

import jax
import jax.numpy as jnp
from jax import lax
from jax.experimental import pallas as pl
from jax.experimental.pallas import tpu as pltpu
from jax.sharding import PartitionSpec as P

HIGHEST = lax.Precision.HIGHEST
TILE = 128
SUB = 8


def lane_of(x, at):
    return jnp.broadcast_to(x[:, at:at + 1], x.shape)


def sub_of(x, at):
    return jnp.broadcast_to(x[at:at + 1, :], x.shape)


def invert_tile(rows):
    shape = rows[0].shape
    lane = lax.broadcasted_iota(jnp.int32, shape, 1)
    sub = lax.broadcasted_iota(jnp.int32, shape, 0)
    count = len(rows)
    diag = [lane_of(rows[0], k) for k in range(SUB)]
    for p in range(count):
        at = SUB * p
        panel = (lane >= at) & (lane < at + SUB)
        more = p + 1 < count
        if more:
            ahead = [lane_of(rows[p + 1], at + SUB + k) for k in range(SUB)]
            near = [lane_of(rows[p + 1], at + k) for k in range(SUB)]
            below = jnp.where(panel, 0.0, rows[p + 1])
        row = jnp.where(panel, jnp.where(lane == sub + at, 1.0, 0.0), rows[p])
        inv, tops, low = [], [], {}
        for k in range(SUB):
            scale = lax.rsqrt(sub_of(diag[k], k))
            inv.append(scale)
            mult = diag[k] * scale
            for j in range(k + 1, SUB):
                low[j, k] = sub_of(diag[j], k) * scale
                diag[j] = diag[j] - mult * low[j, k]
            top = sub_of(row, k) * scale
            tops.append(top)
            row = row - mult * top
            if more:
                side = near[k] * scale
                for j in range(k + 1, SUB):
                    near[j] = near[j] - side * low[j, k]
                for j in range(SUB):
                    ahead[j] = ahead[j] - side * sub_of(side, j)
                below = below - side * top
        done = tops[0]
        for k in range(1, SUB):
            done = jnp.where(sub == k, tops[k], done)
        rows[p] = jnp.where(lane <= sub + at, done, 0.0)
        if more:
            rows[p + 1] = below
            diag = ahead
        for i in range(p + 2, count):
            cols = [lane_of(rows[i], at + k) for k in range(SUB)]
            rest = jnp.where(panel, 0.0, rows[i])
            for k in range(SUB):
                mult = cols[k] * inv[k]
                for j in range(k + 1, SUB):
                    cols[j] = cols[j] - mult * low[j, k]
                rest = rest - mult * tops[k]
            rows[i] = rest
    return jnp.concatenate(rows, axis=0)


def block(i):
    return pl.ds(pl.multiple_of(i * TILE, TILE), TILE)


def factor_in_place(t_ref):
    count = t_ref.shape[0] // TILE

    def step(j, carry):
        here = block(j)
        rows = [
            t_ref[pl.ds(pl.multiple_of(j * TILE + SUB * i, SUB), SUB), here]
            for i in range(TILE // SUB)
        ]
        tile = invert_tile(rows)
        t_ref[here, :] = jnp.dot(tile, t_ref[here, :], precision=HIGHEST)
        t_ref[here, here] = tile

        def below(i, carry):
            there = block(i)
            left = t_ref[here, there]
            t_ref[there, here] = jnp.zeros((TILE, TILE), jnp.float32)
            t_ref[there, :] -= lax.dot_general(
                left, t_ref[here, :], (((0,), (0,)), ((), ())), precision=HIGHEST,
                preferred_element_type=jnp.float32,
            )
            return carry

        return lax.fori_loop(j + 1, count, below, carry)

    lax.fori_loop(0, count, step, 0)


def mask_lower(t_ref):
    order = t_ref.shape[0]
    for j in range(order // TILE - 1):
        t_ref[j * TILE:(j + 1) * TILE, (j + 1) * TILE:] = jnp.zeros(
            (TILE, order - (j + 1) * TILE), jnp.float32
        )


def split(x):
    high = x.astype(jnp.bfloat16)
    return high, (x - high.astype(jnp.float32)).astype(jnp.bfloat16)


def dot3(left, right, dims):
    def one(x, y):
        return lax.dot_general(x, y, (dims, ((), ())), preferred_element_type=jnp.float32)
    return one(left[0], right[1]) + one(left[1], right[0]) + one(left[0], right[0])


NN = ((1,), (0,))
NT = ((1,), (1,))


def tile_home(q, c, core, nb, ncol):
    slab = nb // ncol
    pairs = nb // TILE // 2
    row = c * slab + (q // pairs) * SUB
    col = (q % pairs) * 2 * TILE + core * TILE
    return slice(row, row + SUB), pl.ds(pl.multiple_of(col, TILE), TILE)


def first_kernel(core_ref, own_ref, other_ref, t_ref):
    core = core_ref[0]
    nb = t_ref.shape[0]
    count, ncol = own_ref.shape[:2]
    for q in range(count):
        for c in range(ncol):
            t_ref[tile_home(q, c, core, nb, ncol)] = own_ref[q, c]
            t_ref[tile_home(q, c, 1 - core, nb, ncol)] = other_ref[q, c]
    factor_in_place(t_ref)
    mask_lower(t_ref)


def second_kernel(at_ref, own_ref, other_ref, first_ref, mine_ref, desc_ref,
                  panel_ref, high_ref, low_ref, reduced_ref, var_ref,
                  left_ref, t_ref, x_ref):
    core, prow, pcol = at_ref[0], at_ref[1], at_ref[2]
    nb = t_ref.shape[0]
    qn = x_ref.shape[1]
    count = own_ref.shape[0]
    ncol = nb // SUB // SUB
    for q in range(count):
        for c in range(ncol):
            here = tile_home(q, c, core, nb, ncol)
            there = tile_home(q, c, 1 - core, nb, ncol)
            left_ref[here] = own_ref[q, 2 * c]
            left_ref[there] = other_ref[q, 2 * c]
            t_ref[here] = own_ref[q, 2 * c + 1]
            t_ref[there] = other_ref[q, 2 * c + 1]
        chunk = nb // count // 2
        for t in range(own_ref.shape[1] - 2 * ncol):
            part, tile = divmod(t, chunk // SUB * (qn // TILE))
            row = part * nb + 2 * q * chunk + tile // (qn // TILE) * SUB
            cols = slice(tile % (qn // TILE) * TILE, (tile % (qn // TILE) + 1) * TILE)
            here = pl.ds(pl.multiple_of(row + core * chunk, SUB), SUB)
            there = pl.ds(pl.multiple_of(row + (1 - core) * chunk, SUB), SUB)
            x_ref[here, cols] = own_ref[q, 2 * ncol + t]
            x_ref[there, cols] = other_ref[q, 2 * ncol + t]
    first = first_ref[...]
    left = lax.dot_general(
        left_ref[...], first, (NT, ((), ())), precision=HIGHEST,
        preferred_element_type=jnp.float32,
    )
    left_ref[...] = left
    t_ref[...] -= lax.dot_general(
        left, left, (NT, ((), ())), precision=HIGHEST, preferred_element_type=jnp.float32,
    )
    factor_in_place(t_ref)
    mask_lower(t_ref)
    left_ref[...] = jnp.dot(left_ref[...], first_ref[...], precision=HIGHEST)
    left_ref[...] = -jnp.dot(t_ref[...], left_ref[...], precision=HIGHEST)

    l00 = split(first_ref[...])
    l10 = split(left_ref[...])
    l11 = split(t_ref[...])
    m0 = split(mine_ref[:, :nb])
    m1 = split(mine_ref[:, nb:])
    p0 = dot3(m0, l00, NT)
    p1 = dot3(m0, l10, NT) + dot3(m1, l11, NT)
    row = prow * nb + lax.broadcasted_iota(jnp.int32, (nb, nb), 0)
    col = pcol * nb + lax.broadcasted_iota(jnp.int32, (nb, nb), 1)
    panel_ref[...] = jnp.where(row >= col, jnp.where(pcol == 0, p0, p1), 0.0)
    p0, p1 = split(p0), split(p1)
    w0 = split(dot3(p0, l00, NN) + dot3(p1, l10, NN))
    w1 = split(dot3(p1, l11, NN))
    high_ref[:, :nb] = w0[0]
    low_ref[:, :nb] = w0[1]
    high_ref[:, nb:] = w1[0]
    low_ref[:, nb:] = w1[1]
    x0 = split(x_ref[:nb])
    x1 = split(x_ref[nb:])
    z0 = dot3(l00, x0, NN)
    z1 = dot3(l10, x0, NN) + dot3(l11, x1, NN)
    var_ref[...] = jnp.sum(z0 * z0, axis=0, keepdims=True) + jnp.sum(z1 * z1, axis=0, keepdims=True)
    lowered = desc_ref[...] - (dot3(w0, x0, NN) + dot3(w1, x1, NN))
    reduced_ref[...] = jnp.where(prow == 0, z0, jnp.where(prow == 1, z1, lowered))


VMEM = pl.BlockSpec(memory_space=pltpu.VMEM)
SMEM = pl.BlockSpec(memory_space=pltpu.SMEM)


def factor_first(core, own, other, nb):
    return pl.pallas_call(
        first_kernel,
        out_shape=jax.ShapeDtypeStruct((nb, nb), jnp.float32),
        in_specs=[SMEM, VMEM, VMEM],
        out_specs=VMEM,
        compiler_params=pltpu.CompilerParams(vmem_limit_bytes=24 * 2**20),
        cost_estimate=pl.CostEstimate(flops=150 * nb**3, bytes_accessed=8 * nb * nb, transcendentals=0),
        name="factor_first",
    )(core, own, other)


def factor_second(at, own, other, first, mine, desc):
    nb, order = mine.shape
    qn = desc.shape[1]
    return pl.pallas_call(
        second_kernel,
        out_shape=(
            jax.ShapeDtypeStruct((nb, nb), jnp.float32),
            jax.ShapeDtypeStruct((nb, order), jnp.bfloat16),
            jax.ShapeDtypeStruct((nb, order), jnp.bfloat16),
            jax.ShapeDtypeStruct((nb, qn), jnp.float32),
            jax.ShapeDtypeStruct((1, qn), jnp.float32),
        ),
        in_specs=[SMEM] + [VMEM] * 5,
        out_specs=(VMEM,) * 5,
        scratch_shapes=[pltpu.VMEM((nb, nb), jnp.float32)] * 2 + [pltpu.VMEM((order, qn), jnp.float32)],
        compiler_params=pltpu.CompilerParams(vmem_limit_bytes=32 * 2**20),
        cost_estimate=pl.CostEstimate(flops=300 * nb**3, bytes_accessed=40 * nb * nb, transcendentals=0),
        name="factor_second",
    )(at, own, other, first, mine, desc)


WIDTH = 256


def update_kernel(flip, at_ref, gram_ref, match_ref, high_ref, low_ref, panel_ref, *refs):
    out_ref = refs[-1]
    prow, pcol = at_ref[1], at_ref[2]
    nb = gram_ref.shape[0]
    steps = pl.num_programs(0)
    half = at_ref[0] if not flip else 1 - at_ref[0]
    tile = half * steps + pl.program_id(0)
    is_panel = (pcol < 2) & (tile < nb // WIDTH)

    @pl.when(is_panel)
    def _():
        out_ref[...] = panel_ref[:, pl.ds(pl.multiple_of(tile * WIDTH, WIDTH), WIDTH)]

    @pl.when(jnp.logical_not(is_panel) & (prow < 2))
    def _():
        out_ref[...] = jnp.zeros((nb, WIDTH), jnp.float32)

    @pl.when(jnp.logical_not(is_panel) & (prow >= 2))
    def _():
        match = split(match_ref[...])
        out_ref[...] = gram_ref[...] - dot3((high_ref[...], low_ref[...]), match, NT)


def update(at, gram, match, high, low, panel, done=None):
    nb, stored = gram.shape
    order = high.shape[1]
    steps = stored // 2 // WIDTH
    flip = done is not None

    def place(t, at_ref):
        half = 1 - at_ref[0] if flip else at_ref[0]
        return (0, half * steps + t)

    whole = pl.BlockSpec((nb, order), lambda t, at_ref: (0, 0))
    in_specs = [
        pl.BlockSpec((nb, WIDTH), place),
        pl.BlockSpec((WIDTH, order), lambda t, at_ref: (t, 0)),
        whole, whole, pl.BlockSpec((nb, nb), lambda t, at_ref: (0, 0)),
    ]
    args = [gram, match, high, low, panel]
    if flip:
        in_specs.append(pl.BlockSpec(memory_space=pl.ANY))
        args.append(done)
    return pl.pallas_call(
        functools.partial(update_kernel, flip),
        grid_spec=pltpu.PrefetchScalarGridSpec(
            num_scalar_prefetch=1,
            grid=(steps,),
            in_specs=in_specs,
            out_specs=pl.BlockSpec((nb, WIDTH), place),
        ),
        out_shape=jax.ShapeDtypeStruct((nb, stored), jnp.float32),
        input_output_aliases={6: 0} if flip else {},
        compiler_params=pltpu.CompilerParams(vmem_limit_bytes=20 * 2**20),
        cost_estimate=pl.CostEstimate(
            flops=6 * nb * stored * order // 2, bytes_accessed=4 * nb * stored + 2 * stored * order,
            transcendentals=0,
        ),
        name="update_other" if flip else "update_own",
    )(at, *args)


def spread(x, axis, groups=None):
    size = lax.axis_size(axis) if groups is None else len(groups[0])
    return lax.all_to_all(
        jnp.broadcast_to(x[None], (size,) + x.shape), axis, 0, 0, tiled=True,
        axis_index_groups=groups,
    )


def body(gram, desc):
    nb = gram.shape[0]
    qn = desc.shape[1]
    nrow, ncol = lax.axis_size("row"), lax.axis_size("col")
    groups = nrow // ncol
    order = 2 * nb
    prow = lax.axis_index("row")
    pcol = lax.axis_index("col")
    core = prow % 2
    slab = nb // ncol
    wide = nb // TILE
    lanes = [[2 * q + k for q in range(nrow // 2)] for k in range(2)]
    swap = [(r, r ^ 1) for r in range(nrow)]
    front = gram[:, :nb]

    chunk = nb // nrow
    heads = desc.reshape(nrow, chunk // SUB, SUB, qn // TILE, TILE).transpose(0, 1, 3, 2, 4)
    heads = heads.reshape(nrow, -1, SUB, TILE)
    heads = lax.all_to_all(heads, "row", 0, 0, tiled=True)

    front = front.reshape(ncol, slab, nb)
    slab0 = jnp.where(pcol == 0, front[0], 0.0)
    slab1 = jnp.where(pcol == 1, front[1], 0.0)
    for s in range(1, ncol):
        piece = jnp.where(pcol == 0, front[s], front[(s + 1) % ncol])
        come = lax.ppermute(piece, "col", [(0, s), (1, (s + 1) % ncol)])
        slab0 = jnp.where(pcol == s, come, slab0)
        slab1 = jnp.where(pcol == (s + 1) % ncol, come, slab1)
    heads, slab0, slab1 = lax.optimization_barrier((heads, slab0, slab1))
    rows_slab = jnp.concatenate([slab0, slab1], axis=1)

    mine = lax.all_gather(rows_slab, "col", tiled=True)

    tiles = rows_slab.reshape(slab // SUB, SUB, 2, wide, TILE).transpose(0, 3, 2, 1, 4)
    tiles = tiles.reshape(nrow, 2, SUB, TILE)
    dealt = lax.all_to_all(tiles, "row", 0, 0, tiled=True)

    half = groups // 2
    pairs = []
    for y in range(groups):
        for i in range(ncol):
            for c in range(ncol):
                to = 2 * ((y % half) * ncol + c) + y // half
                pairs.append(((y * ncol + i) * ncol + c, to * ncol + i))
    match = lax.ppermute(rows_slab, ("row", "col"), pairs)

    lead = spread(jnp.concatenate([dealt[0, :1], dealt[1]], axis=0), "col")

    match, lead = lax.optimization_barrier((match, lead))
    lead_own = spread(lead[:, 0], "row", lanes)
    match = lax.all_gather(match, "row", axis_index_groups=lanes, tiled=True)
    lead_other = lax.ppermute(lead_own, "row", swap)
    following = jnp.concatenate(
        [lead[:, 1:].reshape(2 * ncol, SUB, TILE), heads[0], heads[1]], axis=0
    )
    next_own = spread(following, "row", lanes)
    lead_own, mine = lax.optimization_barrier((lead_own, mine))
    index = jnp.stack([core, prow, pcol]).astype(jnp.int32)
    first = factor_first(index, lead_own, lead_other, nb)

    first, next_own = lax.optimization_barrier((first, next_own))
    next_other = lax.ppermute(next_own, "row", swap)
    panel, high, low, reduced, variance = factor_second(
        index, next_own, next_other, first, mine, desc
    )

    high, match = lax.optimization_barrier((high, match))
    other = lax.ppermute(match, "row", swap)
    rest = update(index, gram, match, high, low, panel)
    rest = update(index, gram, other, high, low, panel, rest)
    return (rest, reduced, variance.reshape(qn))


def solution(mesh):
    in_specs = (P("row", "col"), P("row", "col"))
    out_specs = (P("row", "col"), P("row", "col"), P("col"))
    return jax.shard_map(body, mesh=mesh, in_specs=in_specs, out_specs=out_specs, check_vma=False)
```

```python
import functools

import jax
import jax.numpy as jnp
from jax import lax
from jax.experimental import pallas as pl
from jax.experimental.pallas import tpu as pltpu
from jax.sharding import PartitionSpec as P

HIGHEST = lax.Precision.HIGHEST
TILE = 128
SUB = 8


def lane_of(x, at):
    return jnp.broadcast_to(x[:, at:at + 1], x.shape)


def sub_of(x, at):
    return jnp.broadcast_to(x[at:at + 1, :], x.shape)


def invert_tile(rows):
    shape = rows[0].shape
    lane = lax.broadcasted_iota(jnp.int32, shape, 1)
    sub = lax.broadcasted_iota(jnp.int32, shape, 0)
    count = len(rows)
    diag = [lane_of(rows[0], k) for k in range(SUB)]
    for p in range(count):
        at = SUB * p
        panel = (lane >= at) & (lane < at + SUB)
        more = p + 1 < count
        if more:
            ahead = [lane_of(rows[p + 1], at + SUB + k) for k in range(SUB)]
            near = [lane_of(rows[p + 1], at + k) for k in range(SUB)]
            below = jnp.where(panel, 0.0, rows[p + 1])
        row = jnp.where(panel, jnp.where(lane == sub + at, 1.0, 0.0), rows[p])
        inv, tops, low = [], [], {}
        for k in range(SUB):
            scale = lax.rsqrt(sub_of(diag[k], k))
            inv.append(scale)
            mult = diag[k] * scale
            for j in range(k + 1, SUB):
                low[j, k] = sub_of(diag[j], k) * scale
                diag[j] = diag[j] - mult * low[j, k]
            top = sub_of(row, k) * scale
            tops.append(top)
            row = row - mult * top
            if more:
                side = near[k] * scale
                for j in range(k + 1, SUB):
                    near[j] = near[j] - side * low[j, k]
                for j in range(SUB):
                    ahead[j] = ahead[j] - side * sub_of(side, j)
                below = below - side * top
        done = tops[0]
        for k in range(1, SUB):
            done = jnp.where(sub == k, tops[k], done)
        rows[p] = jnp.where(lane <= sub + at, done, 0.0)
        if more:
            rows[p + 1] = below
            diag = ahead
        for i in range(p + 2, count):
            cols = [lane_of(rows[i], at + k) for k in range(SUB)]
            rest = jnp.where(panel, 0.0, rows[i])
            for k in range(SUB):
                mult = cols[k] * inv[k]
                for j in range(k + 1, SUB):
                    cols[j] = cols[j] - mult * low[j, k]
                rest = rest - mult * tops[k]
            rows[i] = rest
    return jnp.concatenate(rows, axis=0)


def block(i):
    return pl.ds(pl.multiple_of(i * TILE, TILE), TILE)


def factor_in_place(t_ref):
    count = t_ref.shape[0] // TILE

    def step(j, carry):
        here = block(j)
        rows = [
            t_ref[pl.ds(pl.multiple_of(j * TILE + SUB * i, SUB), SUB), here]
            for i in range(TILE // SUB)
        ]
        tile = invert_tile(rows)
        t_ref[here, :] = jnp.dot(tile, t_ref[here, :], precision=HIGHEST)
        t_ref[here, here] = tile

        def below(i, carry):
            there = block(i)
            left = t_ref[here, there]
            t_ref[there, here] = jnp.zeros((TILE, TILE), jnp.float32)
            t_ref[there, :] -= lax.dot_general(
                left, t_ref[here, :], (((0,), (0,)), ((), ())), precision=HIGHEST,
                preferred_element_type=jnp.float32,
            )
            return carry

        return lax.fori_loop(j + 1, count, below, carry)

    lax.fori_loop(0, count, step, 0)


def mask_lower(t_ref):
    order = t_ref.shape[0]
    for j in range(order // TILE - 1):
        t_ref[j * TILE:(j + 1) * TILE, (j + 1) * TILE:] = jnp.zeros(
            (TILE, order - (j + 1) * TILE), jnp.float32
        )


def split(x):
    high = x.astype(jnp.bfloat16)
    return high, (x - high.astype(jnp.float32)).astype(jnp.bfloat16)


def dot3(left, right, dims):
    def one(x, y):
        return lax.dot_general(x, y, (dims, ((), ())), preferred_element_type=jnp.float32)
    return one(left[0], right[1]) + one(left[1], right[0]) + one(left[0], right[0])


NN = ((1,), (0,))
NT = ((1,), (1,))


def tile_home(q, c, core, nb, ncol):
    slab = nb // ncol
    pairs = nb // TILE // 2
    row = c * slab + (q // pairs) * SUB
    col = (q % pairs) * 2 * TILE + core * TILE
    return slice(row, row + SUB), pl.ds(pl.multiple_of(col, TILE), TILE)


def first_kernel(core_ref, own_ref, other_ref, t_ref):
    core = core_ref[0]
    nb = t_ref.shape[0]
    count, ncol = own_ref.shape[:2]
    for q in range(count):
        for c in range(ncol):
            t_ref[tile_home(q, c, core, nb, ncol)] = own_ref[q, c]
            t_ref[tile_home(q, c, 1 - core, nb, ncol)] = other_ref[q, c]
    factor_in_place(t_ref)
    mask_lower(t_ref)


def second_kernel(at_ref, own_ref, other_ref, first_ref, mine_ref, desc_ref,
                  panel_ref, high_ref, low_ref, reduced_ref, var_ref,
                  left_ref, t_ref, x_ref):
    core, prow, pcol = at_ref[0], at_ref[1], at_ref[2]
    nb = t_ref.shape[0]
    qn = x_ref.shape[1]
    count = own_ref.shape[0]
    ncol = nb // SUB // SUB
    for q in range(count):
        for c in range(ncol):
            here = tile_home(q, c, core, nb, ncol)
            there = tile_home(q, c, 1 - core, nb, ncol)
            left_ref[here] = own_ref[q, 2 * c]
            left_ref[there] = other_ref[q, 2 * c]
            t_ref[here] = own_ref[q, 2 * c + 1]
            t_ref[there] = other_ref[q, 2 * c + 1]
        chunk = nb // count // 2
        for t in range(own_ref.shape[1] - 2 * ncol):
            part, tile = divmod(t, chunk // SUB * (qn // TILE))
            row = part * nb + 2 * q * chunk + tile // (qn // TILE) * SUB
            cols = slice(tile % (qn // TILE) * TILE, (tile % (qn // TILE) + 1) * TILE)
            here = pl.ds(pl.multiple_of(row + core * chunk, SUB), SUB)
            there = pl.ds(pl.multiple_of(row + (1 - core) * chunk, SUB), SUB)
            x_ref[here, cols] = own_ref[q, 2 * ncol + t]
            x_ref[there, cols] = other_ref[q, 2 * ncol + t]
    first = first_ref[...]
    left = lax.dot_general(
        left_ref[...], first, (NT, ((), ())), precision=HIGHEST,
        preferred_element_type=jnp.float32,
    )
    left_ref[...] = left
    t_ref[...] -= lax.dot_general(
        left, left, (NT, ((), ())), precision=HIGHEST, preferred_element_type=jnp.float32,
    )
    factor_in_place(t_ref)
    mask_lower(t_ref)
    left_ref[...] = jnp.dot(left_ref[...], first_ref[...], precision=HIGHEST)
    left_ref[...] = -jnp.dot(t_ref[...], left_ref[...], precision=HIGHEST)

    l00 = split(first_ref[...])
    l10 = split(left_ref[...])
    l11 = split(t_ref[...])
    m0 = split(mine_ref[:, :nb])
    m1 = split(mine_ref[:, nb:])
    p0 = dot3(m0, l00, NT)
    p1 = dot3(m0, l10, NT) + dot3(m1, l11, NT)
    row = prow * nb + lax.broadcasted_iota(jnp.int32, (nb, nb), 0)
    col = pcol * nb + lax.broadcasted_iota(jnp.int32, (nb, nb), 1)
    panel_ref[...] = jnp.where(row >= col, jnp.where(pcol == 0, p0, p1), 0.0)
    p0, p1 = split(p0), split(p1)
    w0 = split(dot3(p0, l00, NN) + dot3(p1, l10, NN))
    w1 = split(dot3(p1, l11, NN))
    high_ref[:, :nb] = w0[0]
    low_ref[:, :nb] = w0[1]
    high_ref[:, nb:] = w1[0]
    low_ref[:, nb:] = w1[1]
    x0 = split(x_ref[:nb])
    x1 = split(x_ref[nb:])
    z0 = dot3(l00, x0, NN)
    z1 = dot3(l10, x0, NN) + dot3(l11, x1, NN)
    var_ref[...] = jnp.sum(z0 * z0, axis=0, keepdims=True) + jnp.sum(z1 * z1, axis=0, keepdims=True)
    lowered = desc_ref[...] - (dot3(w0, x0, NN) + dot3(w1, x1, NN))
    reduced_ref[...] = jnp.where(prow == 0, z0, jnp.where(prow == 1, z1, lowered))


VMEM = pl.BlockSpec(memory_space=pltpu.VMEM)
SMEM = pl.BlockSpec(memory_space=pltpu.SMEM)


def factor_first(core, own, other, nb):
    return pl.pallas_call(
        first_kernel,
        out_shape=jax.ShapeDtypeStruct((nb, nb), jnp.float32),
        in_specs=[SMEM, VMEM, VMEM],
        out_specs=VMEM,
        compiler_params=pltpu.CompilerParams(vmem_limit_bytes=24 * 2**20),
        cost_estimate=pl.CostEstimate(flops=150 * nb**3, bytes_accessed=8 * nb * nb, transcendentals=0),
        name="factor_first",
    )(core, own, other)


def factor_second(at, own, other, first, mine, desc):
    nb, order = mine.shape
    qn = desc.shape[1]
    return pl.pallas_call(
        second_kernel,
        out_shape=(
            jax.ShapeDtypeStruct((nb, nb), jnp.float32),
            jax.ShapeDtypeStruct((nb, order), jnp.bfloat16),
            jax.ShapeDtypeStruct((nb, order), jnp.bfloat16),
            jax.ShapeDtypeStruct((nb, qn), jnp.float32),
            jax.ShapeDtypeStruct((1, qn), jnp.float32),
        ),
        in_specs=[SMEM] + [VMEM] * 5,
        out_specs=(VMEM,) * 5,
        scratch_shapes=[pltpu.VMEM((nb, nb), jnp.float32)] * 2 + [pltpu.VMEM((order, qn), jnp.float32)],
        compiler_params=pltpu.CompilerParams(vmem_limit_bytes=32 * 2**20),
        cost_estimate=pl.CostEstimate(flops=300 * nb**3, bytes_accessed=40 * nb * nb, transcendentals=0),
        name="factor_second",
    )(at, own, other, first, mine, desc)


WIDTH = 256


def update_kernel(flip, at_ref, gram_ref, match_ref, high_ref, low_ref, panel_ref, *refs):
    out_ref = refs[-1]
    prow, pcol = at_ref[1], at_ref[2]
    nb = gram_ref.shape[0]
    steps = pl.num_programs(0)
    half = at_ref[0] if not flip else 1 - at_ref[0]
    tile = half * steps + pl.program_id(0)
    is_panel = (pcol < 2) & (tile < nb // WIDTH)

    @pl.when(is_panel)
    def _():
        out_ref[...] = panel_ref[:, pl.ds(pl.multiple_of(tile * WIDTH, WIDTH), WIDTH)]

    @pl.when(jnp.logical_not(is_panel) & (prow < 2))
    def _():
        out_ref[...] = jnp.zeros((nb, WIDTH), jnp.float32)

    @pl.when(jnp.logical_not(is_panel) & (prow >= 2))
    def _():
        match = split(match_ref[...])
        out_ref[...] = gram_ref[...] - dot3((high_ref[...], low_ref[...]), match, NT)


def update(at, gram, match, high, low, panel, done=None):
    nb, stored = gram.shape
    order = high.shape[1]
    steps = stored // 2 // WIDTH
    flip = done is not None

    def place(t, at_ref):
        half = 1 - at_ref[0] if flip else at_ref[0]
        return (0, half * steps + t)

    whole = pl.BlockSpec((nb, order), lambda t, at_ref: (0, 0))
    in_specs = [
        pl.BlockSpec((nb, WIDTH), place),
        pl.BlockSpec((WIDTH, order), lambda t, at_ref: (t, 0)),
        whole, whole, pl.BlockSpec((nb, nb), lambda t, at_ref: (0, 0)),
    ]
    args = [gram, match, high, low, panel]
    if flip:
        in_specs.append(pl.BlockSpec(memory_space=pl.ANY))
        args.append(done)
    return pl.pallas_call(
        functools.partial(update_kernel, flip),
        grid_spec=pltpu.PrefetchScalarGridSpec(
            num_scalar_prefetch=1,
            grid=(steps,),
            in_specs=in_specs,
            out_specs=pl.BlockSpec((nb, WIDTH), place),
        ),
        out_shape=jax.ShapeDtypeStruct((nb, stored), jnp.float32),
        input_output_aliases={6: 0} if flip else {},
        compiler_params=pltpu.CompilerParams(vmem_limit_bytes=20 * 2**20),
        cost_estimate=pl.CostEstimate(
            flops=6 * nb * stored * order // 2, bytes_accessed=4 * nb * stored + 2 * stored * order,
            transcendentals=0,
        ),
        name="update_other" if flip else "update_own",
    )(at, *args)


def spread(x, axis, groups=None):
    size = lax.axis_size(axis) if groups is None else len(groups[0])
    return lax.all_to_all(
        jnp.broadcast_to(x[None], (size,) + x.shape), axis, 0, 0, tiled=True,
        axis_index_groups=groups,
    )


def body(gram, desc):
    nb = gram.shape[0]
    qn = desc.shape[1]
    nrow, ncol = lax.axis_size("row"), lax.axis_size("col")
    groups = nrow // ncol
    order = 2 * nb
    prow = lax.axis_index("row")
    pcol = lax.axis_index("col")
    core = prow % 2
    slab = nb // ncol
    wide = nb // TILE
    lanes = [[2 * q + k for q in range(nrow // 2)] for k in range(2)]
    swap = [(r, r ^ 1) for r in range(nrow)]
    front = gram[:, :nb]

    chunk = nb // nrow
    heads = desc.reshape(nrow, chunk // SUB, SUB, qn // TILE, TILE).transpose(0, 1, 3, 2, 4)
    heads = heads.reshape(nrow, -1, SUB, TILE)
    front = front.reshape(ncol, slab, nb)
    slab0 = jnp.where(pcol == 0, front[0], 0.0)
    slab1 = jnp.where(pcol == 1, front[1], 0.0)
    for s in range(1, ncol):
        piece = jnp.where(pcol == 0, front[s], front[(s + 1) % ncol])
        come = lax.ppermute(piece, "col", [(0, s), (1, (s + 1) % ncol)])
        if s == 1:
            come, heads = lax.optimization_barrier((come, heads))
        slab0 = jnp.where(pcol == s, come, slab0)
        slab1 = jnp.where(pcol == (s + 1) % ncol, come, slab1)
    heads = lax.all_to_all(heads, "row", 0, 0, tiled=True)
    heads, slab0, slab1 = lax.optimization_barrier((heads, slab0, slab1))
    rows_slab = jnp.concatenate([slab0, slab1], axis=1)

    mine = lax.all_gather(rows_slab, "col", tiled=True)

    tiles = rows_slab.reshape(slab // SUB, SUB, 2, wide, TILE).transpose(0, 3, 2, 1, 4)
    tiles = tiles.reshape(nrow, 2, SUB, TILE)
    dealt = lax.all_to_all(tiles, "row", 0, 0, tiled=True)

    half = groups // 2
    pairs = []
    for y in range(groups):
        for i in range(ncol):
            for c in range(ncol):
                to = 2 * ((y % half) * ncol + c) + y // half
                pairs.append(((y * ncol + i) * ncol + c, to * ncol + i))
    match = lax.ppermute(rows_slab, ("row", "col"), pairs)

    lead = spread(jnp.concatenate([dealt[0, :1], dealt[1]], axis=0), "col")

    match, lead = lax.optimization_barrier((match, lead))
    lead_own = spread(lead[:, 0], "row", lanes)
    match = lax.all_gather(match, "row", axis_index_groups=lanes, tiled=True)
    lead_other = lax.ppermute(lead_own, "row", swap)
    following = jnp.concatenate(
        [lead[:, 1:].reshape(2 * ncol, SUB, TILE), heads[0], heads[1]], axis=0
    )
    next_own = spread(following, "row", lanes)
    lead_own, mine = lax.optimization_barrier((lead_own, mine))
    index = jnp.stack([core, prow, pcol]).astype(jnp.int32)
    first = factor_first(index, lead_own, lead_other, nb)

    first, next_own = lax.optimization_barrier((first, next_own))
    next_other = lax.ppermute(next_own, "row", swap)
    panel, high, low, reduced, variance = factor_second(
        index, next_own, next_other, first, mine, desc
    )

    high, match = lax.optimization_barrier((high, match))
    other = lax.ppermute(match, "row", swap)
    rest = update(index, gram, match, high, low, panel)
    rest = update(index, gram, other, high, low, panel, rest)
    return (rest, reduced, variance.reshape(qn))


def solution(mesh):
    in_specs = (P("row", "col"), P("row", "col"))
    out_specs = (P("row", "col"), P("row", "col"), P("col"))
    return jax.shard_map(body, mesh=mesh, in_specs=in_specs, out_specs=out_specs, check_vma=False)
```
